128 devices in a mesh: grp: 4 (over y), ctx: 32 (over x, z, core).
Axes of the slice: x: 4, y: 4, z: 4, core: 2. Of those that a mesh axis runs over, the one named last changes fastest.
Arguments:
- queries: bfloat16 [32768, 1024], P(('grp', 'ctx'))
- key_rows: bfloat16 [32768, 128], P(('grp', 'ctx'))
- value_rows: bfloat16 [32768, 128], P(('grp', 'ctx')), may hold values from -6 to 6
- block_place: int32 [256], P(('grp', 'ctx')), may hold values from 0 to 7, as said below
- document_ids: int32 [4, 8192], P('grp', 'ctx'), may hold values from 0 to 64, as said below
Outputs:
- attended: bfloat16 [32768, 1024], P(('grp', 'ctx'))
The draws below stay inside these ranges and needn't reach their ends.
Inputs may be any that keep to these rules, and one draw needn't show every extreme that they name: `block_place`: for each index of ctx, the 4 devices with that index hold together each value 0 .. 7 exactly once: every slot of every context group receives exactly one block, and only from devices with the same ctx index. `document_ids`: along each group's positions the labels never fall, so every document is a run of consecutive positions within one group; no document is longer than 4096 tokens, and every group has one of exactly 4096 tokens.
All inputs are finite; a program needn't handle non-finite values.
Results may differ from the reference program's by a relative error of at most 0.0055.
Values may be sent and summed in bfloat16 or wider, within the bound.
A program may use at most 64 MiB of HBM per device.

```python
import jax
import jax.numpy as jnp
from jax import lax

H = 8
DH = 128
TOK_DEV = 256
BLK = 128
BLKS_DEV = 2
TOKENS = 32768
NBLK = 256
GROUP_TOK = 8192
DOC_MAX = 4096
N_GRP = 4
N_CTX = 32


def draw_queries(key, part):
    key = jax.random.fold_in(key, 3)
    second = jax.random.fold_in(key, 1)
    values = jnp.clip(jax.random.normal(second, (TOKENS, H, DH), jnp.float32), -6.0, 6.0)
    return values.reshape(TOKENS, H * DH).astype(jnp.bfloat16)


def draw_key_rows(key, part):
    key = jax.random.fold_in(key, 4)
    values = jnp.clip(jax.random.normal(key, (TOKENS, DH), jnp.float32), -6.0, 6.0)
    return values.astype(jnp.bfloat16)


def draw_block_place(key, part):
    key = jax.random.fold_in(key, 5)
    column_keys = jax.random.split(key, N_CTX)
    perms = jax.vmap(lambda single: jax.random.permutation(single, N_GRP * BLKS_DEV))(column_keys)
    arranged = perms.reshape(N_CTX, N_GRP, BLKS_DEV).transpose(1, 0, 2).reshape(NBLK)
    return arranged.astype(jnp.int32)


def document_row(key):
    first, second, third = jax.random.split(key, 3)
    start_big = jax.random.randint(first, (), 0, GROUP_TOK - DOC_MAX + 1)
    count = GROUP_TOK // BLK + 1
    after = jax.random.randint(second, (count,), 2 * BLK, DOC_MAX + 1)
    before = jax.random.randint(third, (count,), 2 * BLK, DOC_MAX + 1)
    bounds = jnp.concatenate([jnp.stack([start_big, start_big + DOC_MAX]), start_big + DOC_MAX + jnp.cumsum(after), start_big - jnp.cumsum(before)])
    positions = jnp.arange(GROUP_TOK)
    counted = (bounds[None, :] <= positions[:, None]) & (bounds[None, :] > 0)
    return jnp.sum(counted.astype(jnp.int32), axis=1)


def draw_document_ids(key, part):
    key = jax.random.fold_in(key, 6)
    group_keys = jax.random.split(key, N_GRP)
    labels = jax.vmap(document_row)(group_keys).astype(jnp.int32)
    lifted = (GROUP_TOK // BLK - labels[:, -1]) * (jnp.arange(N_GRP) > 0).astype(jnp.int32)
    return (labels + lifted[:, None]).astype(jnp.int32)


def shard_levels(stream_key, shape, cuts, least, high):
    loudness = 1.0
    for axis_at, blocks in cuts:
        heights = jax.random.uniform(jax.random.fold_in(jax.random.fold_in(stream_key, 6), axis_at), (blocks,), jnp.float32, least / len(cuts), high / len(cuts))
        loudness = loudness * jnp.repeat(jnp.exp(heights), shape[axis_at] // blocks).reshape((-1,) + (1,) * (len(shape) - 1 - axis_at))
    return loudness


def bell_draw(rng, shape, deviation, limit, cuts=(), kind=jnp.bfloat16):
    array = jax.random.normal(rng, shape, jnp.float32) * deviation
    if len(cuts) > 0:
        array = shard_levels(rng, shape, cuts, -0.22, 0.18) * array
    return jnp.clip(array, min=-limit, max=limit).astype(kind)


def setup_inputs(seed: int = 0) -> dict:
    streams_of = jax.random.split(jax.random.key(seed), 6)
    queries = draw_queries(jax.random.fold_in(streams_of[5], 71), 0)
    key_rows = draw_key_rows(jax.random.fold_in(streams_of[5], 71), 0)
    value_rows = bell_draw(streams_of[2], (TOKENS, DH), 1.0, 6.0, ((0, 128),))
    block_place = draw_block_place(jax.random.fold_in(streams_of[5], 71), 0)
    document_ids = draw_document_ids(jax.random.fold_in(streams_of[5], 71), 0)
    return dict(queries=queries, key_rows=key_rows, value_rows=value_rows, block_place=block_place, document_ids=document_ids)


def reference(queries, key_rows, value_rows, block_place, document_ids):
    block_count = TOK_DEV // BLK
    feat_len = H * DH
    scale = DH ** -0.5
    block_ids = jnp.arange(NBLK).astype(jnp.int32)
    rank_ids = ((block_ids // block_count) % N_CTX).astype(jnp.int32)
    place_now = block_place.astype(jnp.int32)
    target = (((place_now // block_count) * N_CTX + rank_ids) * block_count + place_now % block_count).astype(jnp.int32)

    def arrange(rows, width):
        flat = rows.reshape(NBLK, BLK * width)
        moved = jnp.zeros_like(flat).at[target].set(flat)
        return moved.reshape(N_GRP, GROUP_TOK, width)

    group_queries = arrange(queries, feat_len)
    group_keys = arrange(key_rows, DH)
    group_values = arrange(value_rows, DH)
    query_blocks = GROUP_TOK // BLK
    window = min(GROUP_TOK, DOC_MAX + BLK)

    def attend_block(which_block):
        group_at = (which_block // query_blocks).astype(jnp.int32)
        query_first = ((which_block % query_blocks) * BLK).astype(jnp.int32)
        key_first = jnp.maximum(query_first + BLK - window, 0).astype(jnp.int32)
        zero_at = jnp.zeros((), jnp.int32)
        query_part = lax.dynamic_slice(group_queries, (group_at, query_first, zero_at), (1, BLK, feat_len))[0]
        key_part = lax.dynamic_slice(group_keys, (group_at, key_first, zero_at), (1, window, DH))[0]
        value_part = lax.dynamic_slice(group_values, (group_at, key_first, zero_at), (1, window, DH))[0]
        query_docs = lax.dynamic_slice(document_ids, (group_at, query_first), (1, BLK))[0]
        key_docs = lax.dynamic_slice(document_ids, (group_at, key_first), (1, window))[0]
        query_rows = query_part.reshape(BLK * H, DH)
        row_pos = jnp.repeat(query_first + jnp.arange(BLK).astype(jnp.int32), H)
        row_doc = jnp.repeat(query_docs, H)
        key_pos = key_first + jnp.arange(window).astype(jnp.int32)
        scores = jnp.dot(query_rows, key_part.T, preferred_element_type=jnp.float32) * scale
        allowed = (key_pos[None, :] <= row_pos[:, None]) & (key_pos[None, :] >= 0) & (key_docs[None, :] == row_doc[:, None])
        scores = jnp.where(allowed, scores, -jnp.inf)
        row_max = jnp.max(scores, axis=1)
        expo = jnp.exp(scores - row_max[:, None])
        total = jnp.sum(expo, axis=1)
        weights = expo.astype(jnp.bfloat16)
        summed = jnp.dot(weights, value_part, preferred_element_type=jnp.float32)
        return (summed / total[:, None]).astype(jnp.bfloat16).reshape(BLK, feat_len)

    group_out = lax.map(attend_block, jnp.arange(N_GRP * query_blocks).astype(jnp.int32))
    flat_out = group_out.reshape(NBLK, BLK * feat_len)
    return flat_out[target].reshape(TOKENS, feat_len)
```

```python
import functools
import math

import jax
import jax.numpy as jnp
from jax import lax
from jax.experimental import pallas as pl
from jax.experimental.pallas import tpu as pltpu
from jax.sharding import PartitionSpec as P

MESH = pl.DeviceIdType.MESH

DH = 128
BLK = 128
ROWS = 544
AUX = 512
CUT = 272
HALF = {"a": (0, 144, CUT), "b": (CUT, 400, ROWS)}
COLS = 9
BIG = 2.0**126
LOWEST = -3.0e38


def rows_of(part):
    first, _, last = HALF[part]
    return pl.ds(first, last - first)


def kernel(q_ref, k_ref, v_ref, place_ref, docs_ref, out_ref, *scratch):
    bufs = scratch[:COLS]
    qa, kb, vb, acc, top, send_sems, recv_sems = scratch[COLS:]
    y = lax.axis_index("grp")
    rank = lax.axis_index("ctx")
    x, z, core = rank // 8, (rank // 2) % 4, rank % 2
    chip = x * 4 + z

    def device(dx=0, dy=0, dz=0, flip=False):
        to_core = 1 - core if flip else core
        to = (((x + dx + 4) % 4) * 4 + (z + dz + 4) % 4) * 2 + to_core
        return ((y + dy + 4) % 4, to)

    friends = [dict(dx=1), dict(dx=-1), dict(dy=1), dict(dy=-1), dict(dz=1), dict(dz=-1), dict(dz=2), dict(flip=True)]
    barrier = pltpu.get_barrier_semaphore()
    for friend in friends:
        pl.semaphore_signal(barrier, inc=1, device_id=device(**friend), device_id_type=MESH)

    mine = bufs[0]
    mine[core, y, pl.ds(0, 128), :] = k_ref[0:128, :].T
    mine[core, y, pl.ds(128, 128), :] = k_ref[128:256, :].T
    mine[core, y, pl.ds(256, 256), :] = v_ref[...]
    row_at = lax.broadcasted_iota(jnp.int32, (32, 128), 0)
    aux = jnp.where(
        row_at == 0,
        docs_ref[0:1, 0:128],
        jnp.where(
            row_at == 1,
            docs_ref[0:1, 128:256],
            jnp.where(row_at == 2, place_ref[0], jnp.where(row_at == 3, place_ref[1], 0)),
        ),
    )
    mine[core, y, pl.ds(AUX, 32), :] = aux.astype(jnp.float32).astype(jnp.bfloat16)

    index_of = {}

    def sem_at(key):
        return index_of.setdefault(key, len(index_of))

    def active(d):
        return chip >= d

    sent = []

    def copy(key, src_d, dst_d, slot, rows, to):
        at = sem_at(key)
        return pltpu.make_async_remote_copy(
            src_ref=bufs[src_d].at[core, slot, rows, :],
            dst_ref=bufs[dst_d].at[core, slot, rows, :],
            send_sem=send_sems.at[at],
            recv_sem=recv_sems.at[at],
            device_id=to,
            device_id_type=MESH,
        )

    def send(key, src_d, dst_d, slot, rows, to, cond):
        c = copy(key, src_d, dst_d, slot, rows, to)

        @pl.when(cond)
        def _():
            c.start()

        sent.append((c, cond))

    waited = set()

    def receive(key, d, slot, rows, cond):
        if key in waited:
            return
        waited.add(key)
        c = copy(key, d, d, slot, rows, device(dx=1))

        @pl.when(cond)
        def _():
            c.wait_recv()

    def slot_of(k):
        return (y + k + 4) % 4

    def along_y(d, part):
        for step in (1, -1):
            send(("y", d, part, step), d, d, y, rows_of(part), device(dy=step), active(d))

    def half(part, step):
        first, mid, last = HALF[part]
        return pl.ds(first, mid - first) if step == 1 else pl.ds(mid, last - mid)

    def pass_y(d, part):
        for step in (1, -1):
            receive(("y", d, part, step), d, slot_of(-step), rows_of(part), active(d))
            send(("yf", d, part, step), d, d, slot_of(-step), half(part, step), device(dy=step), active(d))

    def last_y(d, part):
        for step in (1, -1):
            receive(("yf", d, part, step), d, slot_of(2), half(part, step), active(d))

    def along_x(d, part, k):
        send(("x", d + 4, part, k), d, d + 4, slot_of(k), rows_of(part), device(dx=1), active(d) & (x <= 2))

    def along_z(d, part, k):
        for delta in (1, 3, 2):
            straight = z + delta <= 3
            to = device(dz=delta)
            for wrap in (False, True):
                dst = d + delta - (4 if wrap else 0)
                if dst < 0 or dst > 7 or dst == 6:
                    continue
                ok = active(d) & (jnp.logical_not(straight) if wrap else straight)
                send(("z", dst, part, k), d, dst, slot_of(k), rows_of(part), to, ok)

    def came_by(d):
        return "x" if d in (4, 8, 6) else "z"

    def forward(d, part, k):
        if d in (0, 4, 2):
            along_x(d, part, k)
        if d in (0, 4, 8):
            along_z(d, part, k)

    def take(d, part, k):
        receive((came_by(d), d, part, k), d, slot_of(k), rows_of(part), active(d))

    def take_a(d):
        take(d, "a", 0)
        along_y(d, "a")
        forward(d, "a", 0)

    def take_b(d):
        for k in (0, 1, -1, 2):
            take(d, "b", k)
            forward(d, "b", k)

    def core_copy(d, slot):
        at = sem_at(("c", d))
        return pltpu.make_async_remote_copy(
            src_ref=bufs[d].at[slot],
            dst_ref=bufs[d].at[slot],
            send_sem=send_sems.at[at],
            recv_sem=recv_sems.at[at],
            device_id=device(flip=True),
            device_id_type=MESH,
        )

    def swap(d):
        c = core_copy(d, core)

        @pl.when(active(d))
        def _():
            c.start()

        sent.append((c, active(d)))

    def swapped(d):
        c = core_copy(d, 1 - core)

        @pl.when(active(d))
        def _():
            c.wait_recv()

    factor = DH**-0.5 * math.log2(math.e)

    def stage(d, j):
        buf = bufs[d]
        group = place_ref[j] // 2
        for c in range(2):
            auxes = [buf[c, i, pl.ds(AUX, 32), :].astype(jnp.float32) for i in range(4)]
            for s in range(2):
                target = (group * 2 + s).astype(jnp.float32)
                keys = jnp.zeros((128, 128), jnp.bfloat16)
                values = jnp.zeros((128, 128), jnp.bfloat16)
                labels = jnp.zeros((1, 128), jnp.float32)
                for i in range(4):
                    labels = jnp.where(group == i, auxes[i][s : s + 1, :], labels)
                    for b in range(2):
                        pick = (auxes[i][2 + b : 3 + b, :] == target).astype(jnp.float32).astype(jnp.bfloat16)
                        keys = keys + buf[c, i, pl.ds(b * 128, 128), :] * pick
                        values = values + buf[c, i, pl.ds(256 + b * 128, 128), :] * pick
                at = (c * 2 + s) * 128
                kb[j, pl.ds(0, 128), pl.ds(at, 128)] = keys
                entry = lax.broadcasted_iota(jnp.int32, (128, 128), 0).astype(jnp.float32)
                kb[j, pl.ds(128, 128), pl.ds(at, 128)] = jnp.where(entry == labels, 0.0, -BIG).astype(jnp.bfloat16)
                vb[j, pl.ds(at, 128), pl.ds(0, 128)] = values

    step_rows = 256

    def attend(d, j):
        stage(d, j)
        slot_now = place_ref[j] % 2

        def body(i, carry):
            at = pl.multiple_of(i * step_rows, step_rows)
            rows = pl.ds(at, step_rows)
            scores = jnp.dot(qa[j, rows, :], kb[j], preferred_element_type=jnp.float32)
            if d == 0:
                q_pos = core * 256 + slot_now * 128 + lax.broadcasted_iota(jnp.int32, (step_rows, 512), 0) % 128
                k_pos = lax.broadcasted_iota(jnp.int32, (step_rows, 512), 1)
                scores = jnp.where(k_pos <= q_pos, scores, -BIG)
            old = top[j, rows, :]
            new = jnp.maximum(old, jnp.max(scores, axis=1, keepdims=True))
            weights = jnp.exp2((scores - new[:, 0:1]) * factor).astype(jnp.bfloat16)
            ratio = jnp.exp2((old - new) * factor)
            got = jnp.dot(weights, vb[j], preferred_element_type=jnp.float32)
            acc[j, rows, 0:128] = acc[j, rows, 0:128] * ratio + got[:, 0:128]
            acc[j, rows, 128:256] = acc[j, rows, 128:256] * ratio + got[:, 128:256]
            top[j, rows, :] = new
            return carry

        lax.fori_loop(0, 1024 // step_rows, body, 0)

    def compute(d):
        @pl.when(active(d))
        def _():
            for j in range(2):
                attend(d, j)

    def ready(d):
        for j in range(2):
            group, s = place_ref[j] // 2, place_ref[j] % 2
            labels = jnp.zeros((1, 128), jnp.float32)
            for i in range(4):
                tile = bufs[0][core, i, pl.ds(AUX, 32), :].astype(jnp.float32)
                for slot in range(2):
                    labels = jnp.where((group == i) & (s == slot), tile[slot : slot + 1, :], labels)
            column = jnp.broadcast_to(labels, (128, 128)).T
            entry = lax.broadcasted_iota(jnp.int32, (128, 128), 1).astype(jnp.float32)
            hot = jnp.where(entry == column, 1.0, 0.0).astype(jnp.bfloat16)
            for h in range(8):
                qa[j, pl.ds(h * 128, 128), pl.ds(128, 128)] = hot

    pl.semaphore_wait(barrier, len(friends))

    along_y(0, "a")
    along_y(0, "b")
    forward(0, "a", 0)
    forward(0, "b", 0)

    for j in range(2):
        for h in range(8):
            qa[j, pl.ds(h * 128, 128), pl.ds(0, 128)] = q_ref[pl.ds(j * 128, 128), pl.ds(h * 128, 128)]
    top[...] = jnp.full(top.shape, LOWEST, jnp.float32)
    acc[...] = jnp.zeros(acc.shape, jnp.float32)
    vb[:, :, pl.ds(128, 128)] = jnp.ones((2, 512, 128), jnp.bfloat16)

    def tail(d):
        last_y(d, "a")
        swap(d)

    pass_y(0, "a")
    pass_y(0, "b")
    forward(0, "b", 1)
    forward(0, "b", -1)
    take_a(4)
    take_a(1)
    take_a(3)
    take_a(2)
    last_y(0, "b")
    forward(0, "b", 2)
    tail(0)
    pass_y(4, "a")
    take_a(8)
    pass_y(1, "a")
    ready(0)
    swapped(0)
    compute(0)
    take_b(4)
    pass_y(3, "a")
    tail(4)
    swapped(4)
    compute(4)
    take_b(1)
    take_a(5)
    pass_y(2, "a")
    tail(1)
    take_a(7)
    take_a(6)
    swapped(1)
    compute(1)
    take_b(3)
    pass_y(8, "a")
    tail(3)
    swapped(3)
    compute(3)
    take_b(2)
    pass_y(5, "a")
    tail(2)
    take_b(8)
    swapped(2)
    compute(2)
    pass_y(7, "a")
    tail(8)
    swapped(8)
    compute(8)
    pass_y(6, "a")
    take_b(5)
    tail(5)
    take_b(7)
    tail(7)
    swapped(5)
    compute(5)
    take_b(6)
    tail(6)
    swapped(7)
    compute(7)
    swapped(6)
    compute(6)

    for j in range(2):
        for h in range(8):
            rows = pl.ds(h * 128, 128)
            result = acc[j, rows, 0:128] / acc[j, rows, 128:256]
            out_ref[pl.ds(j * 128, 128), pl.ds(h * 128, 128)] = result.astype(jnp.bfloat16)

    for c, cond in sent:
        pl.when(cond)(c.wait_send)
    assert len(index_of) <= SEMS, len(index_of)


SEMS = 128


def on_device(queries, key_rows, value_rows, block_place, document_ids):
    vmem = pl.BlockSpec(memory_space=pltpu.VMEM)
    smem = pl.BlockSpec(memory_space=pltpu.SMEM)
    scratch = [pltpu.VMEM((2, 4, ROWS, 128), jnp.bfloat16) for _ in range(COLS)]
    scratch += [
        pltpu.VMEM((2, 1024, 256), jnp.bfloat16),
        pltpu.VMEM((2, 256, 512), jnp.bfloat16),
        pltpu.VMEM((2, 512, 256), jnp.bfloat16),
        pltpu.VMEM((2, 1024, 256), jnp.float32),
        pltpu.VMEM((2, 1024, 128), jnp.float32),
        pltpu.SemaphoreType.DMA((SEMS,)),
        pltpu.SemaphoreType.DMA((SEMS,)),
    ]
    return pl.pallas_call(
        kernel,
        out_shape=jax.ShapeDtypeStruct(queries.shape, jnp.bfloat16),
        in_specs=[vmem, vmem, vmem, smem, vmem],
        out_specs=vmem,
        scratch_shapes=scratch,
        compiler_params=pltpu.CompilerParams(collective_id=0, has_side_effects=True, vmem_limit_bytes=56 * 2**20),
    )(queries, key_rows, value_rows, block_place, document_ids)


def solution(mesh):
    rows = P(("grp", "ctx"), None)
    return jax.shard_map(
        on_device,
        mesh=mesh,
        in_specs=(rows, rows, rows, P(("grp", "ctx")), P("grp", "ctx")),
        out_specs=rows,
        check_vma=False,
    )
```

```python
import functools
import math

import jax
import jax.numpy as jnp
from jax import lax
from jax.experimental import pallas as pl
from jax.experimental.pallas import tpu as pltpu
from jax.sharding import PartitionSpec as P

MESH = pl.DeviceIdType.MESH

DH = 128
BLK = 128
ROWS = 544
AUX = 512
CUT = 272
HALF = {"a": (0, 144, CUT), "b": (CUT, 400, ROWS)}
COLS = 9
BIG = 2.0**126
LOWEST = -3.0e38


def rows_of(part):
    first, _, last = HALF[part]
    return pl.ds(first, last - first)


def kernel(q_ref, k_ref, v_ref, place_ref, docs_ref, out_ref, *scratch):
    bufs = scratch[:COLS]
    qa, kb, vb, acc, top, send_sems, recv_sems = scratch[COLS:]
    y = lax.axis_index("grp")
    rank = lax.axis_index("ctx")
    x, z, core = rank // 8, (rank // 2) % 4, rank % 2
    chip = x * 4 + z

    def device(dx=0, dy=0, dz=0, flip=False):
        to_core = 1 - core if flip else core
        to = (((x + dx + 4) % 4) * 4 + (z + dz + 4) % 4) * 2 + to_core
        return ((y + dy + 4) % 4, to)

    friends = [dict(dx=1), dict(dx=-1), dict(dy=1), dict(dy=-1), dict(dz=1), dict(dz=-1), dict(dz=2), dict(flip=True)]
    barrier = pltpu.get_barrier_semaphore()
    for friend in friends:
        pl.semaphore_signal(barrier, inc=1, device_id=device(**friend), device_id_type=MESH)

    mine = bufs[0]
    mine[core, y, pl.ds(0, 128), :] = k_ref[0:128, :].T
    mine[core, y, pl.ds(128, 128), :] = k_ref[128:256, :].T
    mine[core, y, pl.ds(256, 256), :] = v_ref[...]
    row_at = lax.broadcasted_iota(jnp.int32, (32, 128), 0)
    aux = jnp.where(
        row_at == 0,
        docs_ref[0:1, 0:128],
        jnp.where(
            row_at == 1,
            docs_ref[0:1, 128:256],
            jnp.where(row_at == 2, place_ref[0], jnp.where(row_at == 3, place_ref[1], 0)),
        ),
    )
    mine[core, y, pl.ds(AUX, 32), :] = aux.astype(jnp.float32).astype(jnp.bfloat16)

    index_of = {}

    def sem_at(key):
        return index_of.setdefault(key, len(index_of))

    def active(d):
        return chip >= d

    sent = []

    def copy(key, src_d, dst_d, slot, rows, to):
        at = sem_at(key)
        return pltpu.make_async_remote_copy(
            src_ref=bufs[src_d].at[core, slot, rows, :],
            dst_ref=bufs[dst_d].at[core, slot, rows, :],
            send_sem=send_sems.at[at],
            recv_sem=recv_sems.at[at],
            device_id=to,
            device_id_type=MESH,
        )

    def send(key, src_d, dst_d, slot, rows, to, cond):
        c = copy(key, src_d, dst_d, slot, rows, to)

        @pl.when(cond)
        def _():
            c.start()

        sent.append((c, cond))

    waited = set()

    def receive(key, d, slot, rows, cond):
        if key in waited:
            return
        waited.add(key)
        c = copy(key, d, d, slot, rows, device(dx=1))

        @pl.when(cond)
        def _():
            c.wait_recv()

    def slot_of(k):
        return (y + k + 4) % 4

    def along_y(d, part):
        for step in (1, -1):
            send(("y", d, part, step), d, d, y, rows_of(part), device(dy=step), active(d))

    def half(part, step):
        first, mid, last = HALF[part]
        return pl.ds(first, mid - first) if step == 1 else pl.ds(mid, last - mid)

    def pass_y(d, part):
        for step in (1, -1):
            receive(("y", d, part, step), d, slot_of(-step), rows_of(part), active(d))
            send(("yf", d, part, step), d, d, slot_of(-step), half(part, step), device(dy=step), active(d))

    def last_y(d, part):
        for step in (1, -1):
            receive(("yf", d, part, step), d, slot_of(2), half(part, step), active(d))

    def along_x(d, part, k):
        send(("x", d + 4, part, k), d, d + 4, slot_of(k), rows_of(part), device(dx=1), active(d) & (x <= 2))

    def along_z(d, part, k):
        for delta in (1, 3, 2):
            straight = z + delta <= 3
            to = device(dz=delta)
            for wrap in (False, True):
                dst = d + delta - (4 if wrap else 0)
                if dst < 0 or dst > 7 or dst == 6:
                    continue
                ok = active(d) & (jnp.logical_not(straight) if wrap else straight)
                send(("z", dst, part, k), d, dst, slot_of(k), rows_of(part), to, ok)

    def came_by(d):
        return "x" if d in (4, 8, 6) else "z"

    def forward(d, part, k):
        if d in (0, 4, 2):
            along_x(d, part, k)
        if d in (0, 4, 8):
            along_z(d, part, k)

    def take(d, part, k):
        receive((came_by(d), d, part, k), d, slot_of(k), rows_of(part), active(d))

    def take_a(d):
        take(d, "a", 0)
        along_y(d, "a")
        forward(d, "a", 0)

    def take_b(d):
        for k in (0, 1, -1, 2):
            take(d, "b", k)
            forward(d, "b", k)

    def core_copy(d, slot):
        at = sem_at(("c", d))
        return pltpu.make_async_remote_copy(
            src_ref=bufs[d].at[slot],
            dst_ref=bufs[d].at[slot],
            send_sem=send_sems.at[at],
            recv_sem=recv_sems.at[at],
            device_id=device(flip=True),
            device_id_type=MESH,
        )

    def swap(d):
        c = core_copy(d, core)

        @pl.when(active(d))
        def _():
            c.start()

        sent.append((c, active(d)))

    def swapped(d):
        c = core_copy(d, 1 - core)

        @pl.when(active(d))
        def _():
            c.wait_recv()

    factor = DH**-0.5 * math.log2(math.e)

    def stage(d, j):
        buf = bufs[d]
        group = place_ref[j] // 2
        for c in range(2):
            auxes = [buf[c, i, pl.ds(AUX, 32), :].astype(jnp.float32) for i in range(4)]
            for s in range(2):
                target = (group * 2 + s).astype(jnp.float32)
                keys = jnp.zeros((128, 128), jnp.bfloat16)
                values = jnp.zeros((128, 128), jnp.bfloat16)
                labels = jnp.zeros((1, 128), jnp.float32)
                for i in range(4):
                    labels = jnp.where(group == i, auxes[i][s : s + 1, :], labels)
                    for b in range(2):
                        pick = (auxes[i][2 + b : 3 + b, :] == target).astype(jnp.float32).astype(jnp.bfloat16)
                        keys = keys + buf[c, i, pl.ds(b * 128, 128), :] * pick
                        values = values + buf[c, i, pl.ds(256 + b * 128, 128), :] * pick
                at = (c * 2 + s) * 128
                kb[j, pl.ds(0, 128), pl.ds(at, 128)] = keys
                entry = lax.broadcasted_iota(jnp.int32, (128, 128), 0).astype(jnp.float32)
                kb[j, pl.ds(128, 128), pl.ds(at, 128)] = jnp.where(entry == labels, 0.0, -BIG).astype(jnp.bfloat16)
                vb[j, pl.ds(at, 128), pl.ds(0, 128)] = values

    step_rows = 512

    def attend(d, j):
        stage(d, j)
        slot_now = place_ref[j] % 2

        def score(i):
            rows = pl.ds(i * step_rows, step_rows)
            scores = jnp.dot(qa[j, rows, :], kb[j], preferred_element_type=jnp.float32)
            if d == 0:
                q_pos = core * 256 + slot_now * 128 + lax.broadcasted_iota(jnp.int32, (step_rows, 512), 0) % 128
                k_pos = lax.broadcasted_iota(jnp.int32, (step_rows, 512), 1)
                scores = jnp.where(k_pos <= q_pos, scores, -BIG)
            return scores

        def rest(i, scores):
            rows = pl.ds(i * step_rows, step_rows)
            old = top[j, rows, :]
            new = jnp.maximum(old, jnp.max(scores, axis=1, keepdims=True))
            weights = jnp.exp2((scores - new[:, 0:1]) * factor).astype(jnp.bfloat16)
            ratio = jnp.exp2((old - new) * factor)
            got = jnp.dot(weights, vb[j], preferred_element_type=jnp.float32)
            acc[j, rows, 0:128] = acc[j, rows, 0:128] * ratio + got[:, 0:128]
            acc[j, rows, 128:256] = acc[j, rows, 128:256] * ratio + got[:, 128:256]
            top[j, rows, :] = new

        n = 1024 // step_rows
        now = score(0)
        for i in range(n):
            later = score(i + 1) if i + 1 < n else None
            rest(i, now)
            now = later

    def compute(d):
        @pl.when(active(d))
        def _():
            for j in range(2):
                attend(d, j)

    def ready(d):
        for j in range(2):
            group, s = place_ref[j] // 2, place_ref[j] % 2
            labels = jnp.zeros((1, 128), jnp.float32)
            for i in range(4):
                tile = bufs[0][core, i, pl.ds(AUX, 32), :].astype(jnp.float32)
                for slot in range(2):
                    labels = jnp.where((group == i) & (s == slot), tile[slot : slot + 1, :], labels)
            column = jnp.broadcast_to(labels, (128, 128)).T
            entry = lax.broadcasted_iota(jnp.int32, (128, 128), 1).astype(jnp.float32)
            hot = jnp.where(entry == column, 1.0, 0.0).astype(jnp.bfloat16)
            for h in range(8):
                qa[j, pl.ds(h * 128, 128), pl.ds(128, 128)] = hot

    pl.semaphore_wait(barrier, len(friends))

    along_y(0, "a")
    along_y(0, "b")
    forward(0, "a", 0)
    forward(0, "b", 0)

    for j in range(2):
        for h in range(8):
            qa[j, pl.ds(h * 128, 128), pl.ds(0, 128)] = q_ref[pl.ds(j * 128, 128), pl.ds(h * 128, 128)]
    top[...] = jnp.full(top.shape, LOWEST, jnp.float32)
    acc[...] = jnp.zeros(acc.shape, jnp.float32)
    vb[:, :, pl.ds(128, 128)] = jnp.ones((2, 512, 128), jnp.bfloat16)

    def tail(d):
        last_y(d, "a")
        swap(d)

    pass_y(0, "a")
    pass_y(0, "b")
    forward(0, "b", 1)
    forward(0, "b", -1)
    take_a(4)
    take_a(1)
    take_a(3)
    take_a(2)
    last_y(0, "b")
    forward(0, "b", 2)
    tail(0)
    pass_y(4, "a")
    take_a(8)
    pass_y(1, "a")
    ready(0)
    swapped(0)
    compute(0)
    take_b(4)
    pass_y(3, "a")
    tail(4)
    swapped(4)
    compute(4)
    take_b(1)
    take_a(5)
    pass_y(2, "a")
    tail(1)
    take_a(7)
    take_a(6)
    swapped(1)
    compute(1)
    take_b(3)
    pass_y(8, "a")
    tail(3)
    swapped(3)
    compute(3)
    take_b(2)
    pass_y(5, "a")
    tail(2)
    take_b(8)
    swapped(2)
    compute(2)
    pass_y(7, "a")
    tail(8)
    swapped(8)
    compute(8)
    pass_y(6, "a")
    take_b(5)
    tail(5)
    take_b(7)
    tail(7)
    swapped(5)
    compute(5)
    take_b(6)
    tail(6)
    swapped(7)
    compute(7)
    swapped(6)
    compute(6)

    for j in range(2):
        for h in range(8):
            rows = pl.ds(h * 128, 128)
            result = acc[j, rows, 0:128] / acc[j, rows, 128:256]
            out_ref[pl.ds(j * 128, 128), pl.ds(h * 128, 128)] = result.astype(jnp.bfloat16)

    for c, cond in sent:
        pl.when(cond)(c.wait_send)
    assert len(index_of) <= SEMS, len(index_of)


SEMS = 128


def on_device(queries, key_rows, value_rows, block_place, document_ids):
    vmem = pl.BlockSpec(memory_space=pltpu.VMEM)
    smem = pl.BlockSpec(memory_space=pltpu.SMEM)
    scratch = [pltpu.VMEM((2, 4, ROWS, 128), jnp.bfloat16) for _ in range(COLS)]
    scratch += [
        pltpu.VMEM((2, 1024, 256), jnp.bfloat16),
        pltpu.VMEM((2, 256, 512), jnp.bfloat16),
        pltpu.VMEM((2, 512, 256), jnp.bfloat16),
        pltpu.VMEM((2, 1024, 256), jnp.float32),
        pltpu.VMEM((2, 1024, 128), jnp.float32),
        pltpu.SemaphoreType.DMA((SEMS,)),
        pltpu.SemaphoreType.DMA((SEMS,)),
    ]
    return pl.pallas_call(
        kernel,
        out_shape=jax.ShapeDtypeStruct(queries.shape, jnp.bfloat16),
        in_specs=[vmem, vmem, vmem, smem, vmem],
        out_specs=vmem,
        scratch_shapes=scratch,
        compiler_params=pltpu.CompilerParams(collective_id=0, has_side_effects=True, vmem_limit_bytes=56 * 2**20),
    )(queries, key_rows, value_rows, block_place, document_ids)


def solution(mesh):
    rows = P(("grp", "ctx"), None)
    return jax.shard_map(
        on_device,
        mesh=mesh,
        in_specs=(rows, rows, rows, P(("grp", "ctx")), P("grp", "ctx")),
        out_specs=rows,
        check_vma=False,
    )
```

```python
import functools
import math

import jax
import jax.numpy as jnp
from jax import lax
from jax.experimental import pallas as pl
from jax.experimental.pallas import tpu as pltpu
from jax.sharding import PartitionSpec as P

MESH = pl.DeviceIdType.MESH

DH = 128
BLK = 128
ROWS = 528
AUX = 512
CUT = 256
HALF = {"a": (0, 128, CUT), "b": (CUT, 400, ROWS)}
COLS = 9
BIG = 2.0**126
LOWEST = -3.0e38


ORDER = (
    ("along_y", 0, "b"),
    ("forward", 0, "a", 0),
    ("along_y", 0, "a"),
    ("forward", 0, "b", 0),
    ("take_a", 4),
    ("pass_y", 0, "b"),
    ("pass_y", 0, "a"),
    ("take_b", 4, 0),
    ("pair",),
    ("take_a", 8),
    ("take_b", 1, 0),
    ("take_a", 3),
    ("third",),
    ("take_b", 4, 1),
    ("take_a", 1),
    ("tail", 0, "b"),
    ("pass_y", 4, "a"),
    ("take_b", 3, 0),
    ("take_a", 2),
    ("take_b", 4, -1),
    ("take_b", 4, 2),
    ("take_b", 1, 1),
    ("tail", 0, "a"),
    ("pass_y", 8, "a"),
    ("tail", 4, "b"),
    ("pass_y", 1, "a"),
    ("take_a", 7),
    ("take_b", 8, 1),
    ("take_b", 1, -1),
    ("take_b", 8, 0),
    ("tail", 4, "a"),
    ("comp", (0,), 0),
    ("tail", 1, "a"),
    ("take_a", 5),
    ("tail", 8, "a"),
    ("comp", (0,), 1),
    ("pass_y", 3, "a"),
    ("take_a", 6),
    ("take_b", 1, 2),
    ("take_b", 3, 1),
    ("tail", 1, "b"),
    ("comp", (1, 4), 0),
    ("take_b", 3, 2),
    ("pass_y", 7, "a"),
    ("take_b", 3, -1),
    ("pass_y", 2, "a"),
    ("take_b", 8, -1),
    ("take_b", 5, 1),
    ("take_b", 2, 1),
    ("pass_y", 5, "a"),
    ("tail", 3, "a"),
    ("pass_y", 6, "a"),
    ("take_b", 8, 2),
    ("tail", 8, "b"),
    ("tail", 3, "b"),
    ("take_b", 5, 0),
    ("comp", (1, 4), 1),
    ("take_b", 2, 0),
    ("comp", (3, 8), 0),
    ("take_b", 7, 0),
    ("take_b", 5, 2),
    ("take_b", 5, -1),
    ("tail", 5, "b"),
    ("take_b", 2, -1),
    ("tail", 5, "a"),
    ("comp", (3, 8), 1),
    ("tail", 7, "a"),
    ("take_b", 2, 2),
    ("tail", 2, "a"),
    ("take_b", 7, -1),
    ("comp", (5,), 0),
    ("take_b", 6, -1),
    ("tail", 2, "b"),
    ("tail", 6, "a"),
    ("comp", (5,), 1),
    ("take_b", 6, 0),
    ("take_b", 6, 1),
    ("take_b", 7, 2),
    ("take_b", 6, 2),
    ("tail", 6, "b"),
    ("take_b", 7, 1),
    ("comp", (2,), 0),
    ("tail", 7, "b"),
    ("comp", (2,), 1),
    ("comp", (6, 7), 0),
    ("comp", (6, 7), 1),
)


def rows_of(part):
    first, _, last = HALF[part]
    return pl.ds(first, last - first)


def kernel(q_ref, k_ref, v_ref, place_ref, docs_ref, out_ref, *scratch):
    bufs = scratch[:COLS]
    qa, kb, vb, acc, top, send_sems, recv_sems = scratch[COLS:]
    y = lax.axis_index("grp")
    rank = lax.axis_index("ctx")
    x, z, core = rank // 8, (rank // 2) % 4, rank % 2
    chip = x * 4 + z

    def device(dx=0, dy=0, dz=0, flip=False):
        to_core = 1 - core if flip else core
        to = (((x + dx + 4) % 4) * 4 + (z + dz + 4) % 4) * 2 + to_core
        return ((y + dy + 4) % 4, to)

    friends = [dict(dx=1), dict(dx=-1), dict(dy=1), dict(dy=-1), dict(dz=1), dict(dz=-1), dict(dz=2), dict(flip=True)]
    barrier = pltpu.get_barrier_semaphore()
    for friend in friends:
        pl.semaphore_signal(barrier, inc=1, device_id=device(**friend), device_id_type=MESH)

    mine = bufs[0]
    mine[core, y, pl.ds(0, 128), :] = k_ref[0:128, :].T
    mine[core, y, pl.ds(128, 128), :] = k_ref[128:256, :].T
    mine[core, y, pl.ds(256, 256), :] = v_ref[...]
    row_at = lax.broadcasted_iota(jnp.int32, (16, 128), 0)
    aux = jnp.where(
        row_at == 0,
        docs_ref[0:1, 0:128],
        jnp.where(
            row_at == 1,
            docs_ref[0:1, 128:256],
            jnp.where(row_at == 2, place_ref[0], jnp.where(row_at == 3, place_ref[1], 0)),
        ),
    )
    mine[core, y, pl.ds(AUX, 16), :] = aux.astype(jnp.float32).astype(jnp.bfloat16)

    index_of = {}

    def sem_at(key):
        return index_of.setdefault(key, len(index_of))

    def active(d):
        return chip >= d

    sent = []

    def copy(key, src_d, dst_d, slot, rows, to):
        at = sem_at(key)
        return pltpu.make_async_remote_copy(
            src_ref=bufs[src_d].at[core, slot, rows, :],
            dst_ref=bufs[dst_d].at[core, slot, rows, :],
            send_sem=send_sems.at[at],
            recv_sem=recv_sems.at[at],
            device_id=to,
            device_id_type=MESH,
        )

    def send(key, src_d, dst_d, slot, rows, to, cond):
        c = copy(key, src_d, dst_d, slot, rows, to)

        @pl.when(cond)
        def _():
            c.start()

        sent.append((c, cond))

    waited = set()

    def receive(key, d, slot, rows, cond):
        if key in waited:
            return
        waited.add(key)
        c = copy(key, d, d, slot, rows, device(dx=1))

        @pl.when(cond)
        def _():
            c.wait_recv()

    def slot_of(k):
        return (y + k + 4) % 4

    def along_y(d, part):
        for step in (1, -1):
            send(("y", d, part, step), d, d, y, rows_of(part), device(dy=step), active(d))

    def half(part, step):
        first, mid, last = HALF[part]
        return pl.ds(first, mid - first) if step == 1 else pl.ds(mid, last - mid)

    def pass_y(d, part):
        for step in (1, -1):
            receive(("y", d, part, step), d, slot_of(-step), rows_of(part), active(d))
            send(("yf", d, part, step), d, d, slot_of(-step), half(part, step), device(dy=step), active(d))

    def last_y(d, part):
        for step in (1, -1):
            receive(("yf", d, part, step), d, slot_of(2), half(part, step), active(d))

    def along_x(d, part, k):
        send(("x", d + 4, part, k), d, d + 4, slot_of(k), rows_of(part), device(dx=1), active(d) & (x <= 2))

    def along_z(d, part, k):
        for delta in (1, 3, 2):
            straight = z + delta <= 3
            to = device(dz=delta)
            for wrap in (False, True):
                dst = d + delta - (4 if wrap else 0)
                if dst < 0 or dst > 7 or dst == 6:
                    continue
                ok = active(d) & (jnp.logical_not(straight) if wrap else straight)
                send(("z", dst, part, k), d, dst, slot_of(k), rows_of(part), to, ok)

    def came_by(d):
        return "x" if d in (4, 8, 6) else "z"

    def forward(d, part, k):
        if d in (0, 4, 2):
            along_x(d, part, k)
        if d in (0, 4, 8):
            along_z(d, part, k)

    def take(d, part, k):
        receive((came_by(d), d, part, k), d, slot_of(k), rows_of(part), active(d))

    def take_a(d):
        take(d, "a", 0)
        along_y(d, "a")
        forward(d, "a", 0)

    def take_b(d, k):
        take(d, "b", k)
        forward(d, "b", k)

    def core_copy(d, part, slot):
        at = sem_at(("c", d, part))
        piece = bufs[d].at[slot, :, rows_of(part), :]
        return pltpu.make_async_remote_copy(
            src_ref=piece,
            dst_ref=piece,
            send_sem=send_sems.at[at],
            recv_sem=recv_sems.at[at],
            device_id=device(flip=True),
            device_id_type=MESH,
        )

    def swap(d, part):
        c = core_copy(d, part, core)

        @pl.when(active(d))
        def _():
            c.start()

        sent.append((c, active(d)))

    def swapped(d):
        for part in ("a", "b"):
            c = core_copy(d, part, 1 - core)
            pl.when(active(d))(c.wait_recv)

    factor = DH**-0.5 * math.log2(math.e)

    def stage(d, base):
        buf = bufs[d]
        groups = [place_ref[j] // 2 for j in range(2)]
        entry = lax.broadcasted_iota(jnp.int32, (128, 128), 0).astype(jnp.float32)
        for c in range(2):
            auxes = [buf[c, i, pl.ds(AUX, 16), :].astype(jnp.float32) for i in range(4)]
            wanted = [(j, s) for j in range(2) for s in range(2)]
            picks = {}
            for i in range(4):
                for b in range(2):
                    place = auxes[i][2 + b : 3 + b, :]
                    for j, s in wanted:
                        hit = place == (groups[j] * 2 + s).astype(jnp.float32)
                        picks[i, b, j, s] = hit.astype(jnp.float32).astype(jnp.bfloat16)
            for first, ref in ((0, kb), (256, vb)):
                found = {w: None for w in wanted}
                for i in range(4):
                    for b in range(2):
                        block = buf[c, i, pl.ds(first + b * 128, 128), :]
                        for w in wanted:
                            term = block * picks[(i, b) + w]
                            found[w] = term if found[w] is None else found[w] + term
                for j, s in wanted:
                    at = pl.ds(base + (c * 2 + s) * 128, 128)
                    if first == 0:
                        kb[j, pl.ds(0, 128), at] = found[j, s]
                    else:
                        vb[j, at, pl.ds(0, 128)] = found[j, s]
            for j, s in wanted:
                labels = auxes[0][s : s + 1, :]
                for i in range(1, 4):
                    labels = jnp.where(groups[j] == i, auxes[i][s : s + 1, :], labels)
                at = pl.ds(base + (c * 2 + s) * 128, 128)
                kb[j, pl.ds(128, 128), at] = jnp.where(entry == labels, 0.0, -BIG).astype(jnp.bfloat16)

    step_rows = 512

    def attend(ds, j):
        n_keys = 512 * len(ds)

        def score(i):
            rows = pl.ds(i * step_rows, step_rows)
            scores = jnp.dot(qa[j, rows, :], kb[j, :, 0:n_keys], preferred_element_type=jnp.float32)
            if 0 in ds:
                q_pos = core * 256 + (place_ref[j] % 2) * 128 + lax.broadcasted_iota(jnp.int32, (step_rows, n_keys), 0) % 128
                k_pos = lax.broadcasted_iota(jnp.int32, (step_rows, n_keys), 1)
                scores = jnp.where(k_pos <= q_pos, scores, -BIG)
            return scores

        def rest(i, scores):
            rows = pl.ds(i * step_rows, step_rows)
            old = top[j, rows, :]
            new = jnp.maximum(old, jnp.max(scores, axis=1, keepdims=True))
            weights = jnp.exp2((scores - new[:, 0:1]) * factor).astype(jnp.bfloat16)
            ratio = jnp.exp2((old - new) * factor)
            got = jnp.dot(weights, vb[j, 0:n_keys, :], preferred_element_type=jnp.float32)
            acc[j, rows, 0:128] = acc[j, rows, 0:128] * ratio + got[:, 0:128]
            acc[j, rows, 128:256] = acc[j, rows, 128:256] * ratio + got[:, 128:256]
            top[j, rows, :] = new

        n = 1024 // step_rows
        now = score(0)
        for i in range(n):
            later = score(i + 1) if i + 1 < n else None
            rest(i, now)
            now = later

    def compute(ds, j):
        def some(ds):
            if j == 0:
                for e, d in enumerate(ds):
                    stage(d, 512 * e)
            attend(ds, j)

        if len(ds) == 1:
            pl.when(active(ds[0]))(lambda: some(ds))
        else:
            pl.when(active(ds[1]))(lambda: some(ds))
            pl.when(active(ds[0]) & jnp.logical_not(active(ds[1])))(lambda: some(ds[:1]))

    def ready():
        for j in range(2):
            group, s = place_ref[j] // 2, place_ref[j] % 2
            labels = jnp.zeros((1, 128), jnp.float32)
            for i in range(4):
                tile = bufs[0][core, i, pl.ds(AUX, 16), :].astype(jnp.float32)
                for slot in range(2):
                    labels = jnp.where((group == i) & (s == slot), tile[slot : slot + 1, :], labels)
            column = jnp.broadcast_to(labels, (128, 128)).T
            entry = lax.broadcasted_iota(jnp.int32, (128, 128), 1).astype(jnp.float32)
            hot = jnp.where(entry == column, 1.0, 0.0).astype(jnp.bfloat16)
            for h in range(8):
                qa[j, pl.ds(h * 128, 128), pl.ds(128, 128)] = hot

    pl.semaphore_wait(barrier, len(friends))

    def local():
        for j in range(2):
            for h in range(8):
                qa[j, pl.ds(h * 128, 128), pl.ds(0, 128)] = q_ref[pl.ds(j * 128, 128), pl.ds(h * 128, 128)]
        top[...] = jnp.full(top.shape, LOWEST, jnp.float32)
        acc[...] = jnp.zeros(acc.shape, jnp.float32)
        vb[:, :, pl.ds(128, 128)] = jnp.ones((2, 1024, 128), jnp.bfloat16)

    def tail(d, part):
        if part == "a":
            last_y(d, "a")
        swap(d, part)

    def pair():
        forward(0, "b", 1)
        forward(0, "b", -1)

    def third():
        last_y(0, "b")
        forward(0, "b", 2)

    def comp(ds, j):
        if j == 0:
            for d in ds:
                swapped(d)
            if 0 in ds:
                ready()
        compute(ds, j)

    steps = dict(
        along_y=along_y, pass_y=pass_y, forward=forward, take_a=take_a, take_b=take_b, tail=tail, pair=pair, third=third, comp=comp
    )
    for at, (name, *args) in enumerate(ORDER):
        if at == 4:
            local()
        steps[name](*args)

    for j in range(2):
        for h in range(8):
            rows = pl.ds(h * 128, 128)
            result = acc[j, rows, 0:128] / acc[j, rows, 128:256]
            out_ref[pl.ds(j * 128, 128), pl.ds(h * 128, 128)] = result.astype(jnp.bfloat16)

    for c, cond in sent:
        pl.when(cond)(c.wait_send)
    assert len(index_of) <= SEMS, len(index_of)


SEMS = 128


def on_device(queries, key_rows, value_rows, block_place, document_ids):
    vmem = pl.BlockSpec(memory_space=pltpu.VMEM)
    smem = pl.BlockSpec(memory_space=pltpu.SMEM)
    scratch = [pltpu.VMEM((2, 4, ROWS, 128), jnp.bfloat16) for _ in range(COLS)]
    scratch += [
        pltpu.VMEM((2, 1024, 256), jnp.bfloat16),
        pltpu.VMEM((2, 256, 1024), jnp.bfloat16),
        pltpu.VMEM((2, 1024, 256), jnp.bfloat16),
        pltpu.VMEM((2, 1024, 256), jnp.float32),
        pltpu.VMEM((2, 1024, 128), jnp.float32),
        pltpu.SemaphoreType.DMA((SEMS,)),
        pltpu.SemaphoreType.DMA((SEMS,)),
    ]
    return pl.pallas_call(
        kernel,
        out_shape=jax.ShapeDtypeStruct(queries.shape, jnp.bfloat16),
        in_specs=[vmem, vmem, vmem, smem, vmem],
        out_specs=vmem,
        scratch_shapes=scratch,
        compiler_params=pltpu.CompilerParams(collective_id=0, has_side_effects=True, vmem_limit_bytes=56 * 2**20),
    )(queries, key_rows, value_rows, block_place, document_ids)


def solution(mesh):
    rows = P(("grp", "ctx"), None)
    return jax.shard_map(
        on_device,
        mesh=mesh,
        in_specs=(rows, rows, rows, P(("grp", "ctx")), P("grp", "ctx")),
        out_specs=rows,
        check_vma=False,
    )
```

```python
import functools
import math

import jax
import jax.numpy as jnp
from jax import lax
from jax.experimental import pallas as pl
from jax.experimental.pallas import tpu as pltpu
from jax.sharding import PartitionSpec as P

MESH = pl.DeviceIdType.MESH

DH = 128
BLK = 128
ROWS = 528
AUX = 512
CUT = 256
HALF = {"a": (0, 128, CUT), "b": (CUT, 400, ROWS)}
COLS = 9
BIG = 2.0**126
LOWEST = -3.0e38


ORDER = (
    ("forward", 0, "a", 0),
    ("along_y", 0, "a"),
    ("forward", 0, "b", 0),
    ("along_y", 0, "b"),
    ("take_a", 4),
    ("pass_y", 0, "b"),
    ("pair",),
    ("take_b", 4, 0),
    ("take_a", 8),
    ("take_a", 1),
    ("pass_y", 0, "a"),
    ("third",),
    ("take_b", 1, 0),
    ("pass_y", 4, "a"),
    ("take_b", 4, -1),
    ("take_b", 4, 1),
    ("tail", 0, "b"),
    ("pass_y", 1, "a"),
    ("tail", 0, "a"),
    ("take_a", 3),
    ("tail", 4, "a"),
    ("take_b", 3, 0),
    ("take_b", 4, 2),
    ("tail", 1, "a"),
    ("tail", 4, "b"),
    ("comp", (0,), 0),
    ("take_b", 1, 1),
    ("take_a", 7),
    ("take_b", 8, 0),
    ("pass_y", 8, "a"),
    ("take_a", 5),
    ("take_b", 1, -1),
    ("pass_y", 3, "a"),
    ("take_a", 2),
    ("comp", (0,), 1),
    ("take_b", 1, 2),
    ("tail", 1, "b"),
    ("take_b", 8, 1),
    ("take_b", 8, 2),
    ("take_b", 3, -1),
    ("comp", (1, 4), 0),
    ("take_b", 3, 1),
    ("tail", 3, "a"),
    ("take_b", 8, -1),
    ("pass_y", 5, "a"),
    ("tail", 8, "a"),
    ("take_b", 3, 2),
    ("take_a", 6),
    ("pass_y", 7, "a"),
    ("tail", 3, "b"),
    ("tail", 8, "b"),
    ("pass_y", 2, "a"),
    ("take_b", 2, -1),
    ("take_b", 7, 0),
    ("comp", (1, 4), 1),
    ("take_b", 7, 1),
    ("take_b", 2, 0),
    ("take_b", 2, 1),
    ("take_b", 5, 2),
    ("take_b", 5, 1),
    ("take_b", 5, 0),
    ("comp", (3, 8), 0),
    ("take_b", 5, -1),
    ("take_b", 6, -1),
    ("take_b", 7, 2),
    ("take_b", 2, 2),
    ("tail", 2, "a"),
    ("take_b", 6, 0),
    ("tail", 5, "a"),
    ("tail", 5, "b"),
    ("pass_y", 6, "a"),
    ("comp", (3, 8), 1),
    ("take_b", 7, -1),
    ("tail", 7, "b"),
    ("take_b", 6, 1),
    ("tail", 2, "b"),
    ("comp", (5,), 0),
    ("take_b", 6, 2),
    ("tail", 6, "a"),
    ("comp", (5,), 1),
    ("tail", 7, "a"),
    ("tail", 6, "b"),
    ("comp", (2,), 0),
    ("comp", (2,), 1),
    ("comp", (6, 7), 0),
    ("comp", (6, 7), 1),
)


def rows_of(part):
    first, _, last = HALF[part]
    return pl.ds(first, last - first)


def kernel(q_ref, k_ref, v_ref, place_ref, docs_ref, out_ref, *scratch):
    bufs = scratch[:COLS]
    qa, kb, vb, acc, top, send_sems, recv_sems = scratch[COLS:]
    y = lax.axis_index("grp")
    rank = lax.axis_index("ctx")
    x, z, core = lax.div(rank, 8), lax.rem(lax.div(rank, 2), 4), lax.rem(rank, 2)
    chip = x * 4 + z

    xs, ys, zs = ([lax.rem(v + k, 4) for k in range(4)] for v in (x, y, z))
    here = {(a, c): (xs[a] * 4 + zs[c]) * 2 + core for a, c in ((0, 0), (1, 0), (3, 0), (0, 1), (0, 2), (0, 3))}
    partner = chip * 2 + 1 - core

    def device(dx=0, dy=0, dz=0, flip=False):
        return (ys[dy % 4], partner if flip else here[dx % 4, dz % 4])

    friends = [dict(dx=1), dict(dx=-1), dict(dy=1), dict(dy=-1), dict(dz=1), dict(dz=-1), dict(dz=2), dict(flip=True)]
    barrier = pltpu.get_barrier_semaphore()
    for friend in friends:
        pl.semaphore_signal(barrier, inc=1, device_id=device(**friend), device_id_type=MESH)

    mine = bufs[0]
    mine[core, y, pl.ds(0, 128), :] = k_ref[0:128, :].T
    mine[core, y, pl.ds(128, 128), :] = k_ref[128:256, :].T
    mine[core, y, pl.ds(256, 256), :] = v_ref[...]
    row_at = lax.broadcasted_iota(jnp.int32, (16, 128), 0)
    aux = jnp.where(
        row_at == 0,
        docs_ref[0:1, 0:128],
        jnp.where(
            row_at == 1,
            docs_ref[0:1, 128:256],
            jnp.where(row_at == 2, place_ref[0], jnp.where(row_at == 3, place_ref[1], 0)),
        ),
    )
    mine[core, y, pl.ds(AUX, 16), :] = aux.astype(jnp.float32).astype(jnp.bfloat16)

    index_of = {}

    def sem_at(key):
        return index_of.setdefault(key, len(index_of))

    def active(d):
        return chip >= d

    sent = []

    def copy(key, src_d, dst_d, slot, rows, to):
        at = sem_at(key)
        return pltpu.make_async_remote_copy(
            src_ref=bufs[src_d].at[core, slot, rows, :],
            dst_ref=bufs[dst_d].at[core, slot, rows, :],
            send_sem=send_sems.at[at],
            recv_sem=recv_sems.at[at],
            device_id=to,
            device_id_type=MESH,
        )

    def send(key, src_d, dst_d, slot, rows, to, cond):
        c = copy(key, src_d, dst_d, slot, rows, to)

        @pl.when(cond)
        def _():
            c.start()

        sent.append((c, cond))

    waited = set()

    def receive(key, d, slot, rows, cond):
        if key in waited:
            return
        waited.add(key)
        c = copy(key, d, d, slot, rows, device(dx=1))

        @pl.when(cond)
        def _():
            c.wait_recv()

    def slot_of(k):
        return ys[k % 4]

    def along_y(d, part):
        for step in (1, -1):
            send(("y", d, part, step), d, d, y, rows_of(part), device(dy=step), active(d))

    def half(part, step):
        first, mid, last = HALF[part]
        return pl.ds(first, mid - first) if step == 1 else pl.ds(mid, last - mid)

    def pass_y(d, part):
        for step in (1, -1):
            receive(("y", d, part, step), d, slot_of(-step), rows_of(part), active(d))
            send(("yf", d, part, step), d, d, slot_of(-step), half(part, step), device(dy=step), active(d))

    def last_y(d, part):
        for step in (1, -1):
            receive(("yf", d, part, step), d, slot_of(2), half(part, step), active(d))

    def along_x(d, part, k):
        send(("x", d + 4, part, k), d, d + 4, slot_of(k), rows_of(part), device(dx=1), active(d) & (x <= 2))

    def along_z(d, part, k):
        for delta in (1, 3, 2):
            straight = z + delta <= 3
            to = device(dz=delta)
            for wrap in (False, True):
                dst = d + delta - (4 if wrap else 0)
                if dst < 0 or dst > 7 or dst == 6:
                    continue
                ok = active(d) & (jnp.logical_not(straight) if wrap else straight)
                send(("z", dst, part, k), d, dst, slot_of(k), rows_of(part), to, ok)

    def came_by(d):
        return "x" if d in (4, 8, 6) else "z"

    def forward(d, part, k):
        if d in (0, 4, 2):
            along_x(d, part, k)
        if d in (0, 4, 8):
            along_z(d, part, k)

    def take(d, part, k):
        receive((came_by(d), d, part, k), d, slot_of(k), rows_of(part), active(d))

    def take_a(d):
        take(d, "a", 0)
        along_y(d, "a")
        forward(d, "a", 0)

    def take_b(d, k):
        take(d, "b", k)
        forward(d, "b", k)

    def core_copy(d, part, slot):
        at = sem_at(("c", d, part))
        piece = bufs[d].at[slot, :, rows_of(part), :]
        return pltpu.make_async_remote_copy(
            src_ref=piece,
            dst_ref=piece,
            send_sem=send_sems.at[at],
            recv_sem=recv_sems.at[at],
            device_id=device(flip=True),
            device_id_type=MESH,
        )

    def swap(d, part):
        c = core_copy(d, part, core)

        @pl.when(active(d))
        def _():
            c.start()

        sent.append((c, active(d)))

    def swapped(d):
        for part in ("a", "b"):
            c = core_copy(d, part, 1 - core)
            pl.when(active(d))(c.wait_recv)

    factor = DH**-0.5 * math.log2(math.e)

    def stage(d, base):
        buf = bufs[d]
        groups = [place_ref[j] // 2 for j in range(2)]
        entry = lax.broadcasted_iota(jnp.int32, (128, 128), 0).astype(jnp.float32)
        for c in range(2):
            auxes = [buf[c, i, pl.ds(AUX, 16), :].astype(jnp.float32) for i in range(4)]
            wanted = [(j, s) for j in range(2) for s in range(2)]
            picks = {}
            for i in range(4):
                for b in range(2):
                    place = auxes[i][2 + b : 3 + b, :]
                    for j, s in wanted:
                        hit = place == (groups[j] * 2 + s).astype(jnp.float32)
                        picks[i, b, j, s] = hit.astype(jnp.float32).astype(jnp.bfloat16)
            for first, ref in ((0, kb), (256, vb)):
                found = {w: None for w in wanted}
                for i in range(4):
                    for b in range(2):
                        block = buf[c, i, pl.ds(first + b * 128, 128), :]
                        for w in wanted:
                            term = block * picks[(i, b) + w]
                            found[w] = term if found[w] is None else found[w] + term
                for j, s in wanted:
                    at = pl.ds(base + (c * 2 + s) * 128, 128)
                    if first == 0:
                        kb[j, pl.ds(0, 128), at] = found[j, s]
                    else:
                        vb[j, at, pl.ds(0, 128)] = found[j, s]
            for j, s in wanted:
                labels = auxes[0][s : s + 1, :]
                for i in range(1, 4):
                    labels = jnp.where(groups[j] == i, auxes[i][s : s + 1, :], labels)
                at = pl.ds(base + (c * 2 + s) * 128, 128)
                kb[j, pl.ds(128, 128), at] = jnp.where(entry == labels, 0.0, -BIG).astype(jnp.bfloat16)

    step_rows = 512

    def attend(ds, j):
        n_keys = 512 * len(ds)

        def score(i):
            rows = pl.ds(i * step_rows, step_rows)
            scores = jnp.dot(qa[j, rows, :], kb[j, :, 0:n_keys], preferred_element_type=jnp.float32)
            if 0 in ds:
                q_pos = core * 256 + (place_ref[j] % 2) * 128 + lax.broadcasted_iota(jnp.int32, (step_rows, n_keys), 0) % 128
                k_pos = lax.broadcasted_iota(jnp.int32, (step_rows, n_keys), 1)
                scores = jnp.where(k_pos <= q_pos, scores, -BIG)
            return scores

        def rest(i, scores):
            rows = pl.ds(i * step_rows, step_rows)
            old = top[j, rows, :]
            new = jnp.maximum(old, jnp.max(scores, axis=1, keepdims=True))
            weights = jnp.exp2((scores - new[:, 0:1]) * factor).astype(jnp.bfloat16)
            ratio = jnp.exp2((old - new) * factor)
            got = jnp.dot(weights, vb[j, 0:n_keys, :], preferred_element_type=jnp.float32)
            acc[j, rows, 0:128] = acc[j, rows, 0:128] * ratio + got[:, 0:128]
            acc[j, rows, 128:256] = acc[j, rows, 128:256] * ratio + got[:, 128:256]
            top[j, rows, :] = new

        n = 1024 // step_rows
        now = score(0)
        for i in range(n):
            later = score(i + 1) if i + 1 < n else None
            rest(i, now)
            now = later

    def compute(ds, j):
        def some(ds):
            if j == 0:
                for e, d in enumerate(ds):
                    stage(d, 512 * e)
            attend(ds, j)

        if len(ds) == 1:
            pl.when(active(ds[0]))(lambda: some(ds))
        else:
            pl.when(active(ds[1]))(lambda: some(ds))
            pl.when(active(ds[0]) & jnp.logical_not(active(ds[1])))(lambda: some(ds[:1]))

    def ready():
        for j in range(2):
            group, s = place_ref[j] // 2, place_ref[j] % 2
            labels = jnp.zeros((1, 128), jnp.float32)
            for i in range(4):
                tile = bufs[0][core, i, pl.ds(AUX, 16), :].astype(jnp.float32)
                for slot in range(2):
                    labels = jnp.where((group == i) & (s == slot), tile[slot : slot + 1, :], labels)
            column = jnp.broadcast_to(labels, (128, 128)).T
            entry = lax.broadcasted_iota(jnp.int32, (128, 128), 1).astype(jnp.float32)
            hot = jnp.where(entry == column, 1.0, 0.0).astype(jnp.bfloat16)
            for h in range(8):
                qa[j, pl.ds(h * 128, 128), pl.ds(128, 128)] = hot

    pl.semaphore_wait(barrier, len(friends))

    def local():
        for j in range(2):
            for h in range(8):
                qa[j, pl.ds(h * 128, 128), pl.ds(0, 128)] = q_ref[pl.ds(j * 128, 128), pl.ds(h * 128, 128)]
        top[...] = jnp.full(top.shape, LOWEST, jnp.float32)
        acc[...] = jnp.zeros(acc.shape, jnp.float32)
        vb[:, :, pl.ds(128, 128)] = jnp.ones((2, 1024, 128), jnp.bfloat16)

    def tail(d, part):
        if part == "a":
            last_y(d, "a")
        swap(d, part)

    def pair():
        forward(0, "b", 1)
        forward(0, "b", -1)

    def third():
        last_y(0, "b")
        forward(0, "b", 2)

    def comp(ds, j):
        if j == 0:
            for d in ds:
                swapped(d)
            if 0 in ds:
                ready()
        compute(ds, j)

    steps = dict(
        along_y=along_y, pass_y=pass_y, forward=forward, take_a=take_a, take_b=take_b, tail=tail, pair=pair, third=third, comp=comp
    )
    for at, (name, *args) in enumerate(ORDER):
        if at == 4:
            local()
        steps[name](*args)

    for j in range(2):
        for h in range(8):
            rows = pl.ds(h * 128, 128)
            result = acc[j, rows, 0:128] / acc[j, rows, 128:256]
            out_ref[pl.ds(j * 128, 128), pl.ds(h * 128, 128)] = result.astype(jnp.bfloat16)

    for c, cond in sent:
        pl.when(cond)(c.wait_send)
    assert len(index_of) <= SEMS, len(index_of)


SEMS = 128


def on_device(queries, key_rows, value_rows, block_place, document_ids):
    vmem = pl.BlockSpec(memory_space=pltpu.VMEM)
    smem = pl.BlockSpec(memory_space=pltpu.SMEM)
    scratch = [pltpu.VMEM((2, 4, ROWS, 128), jnp.bfloat16) for _ in range(COLS)]
    scratch += [
        pltpu.VMEM((2, 1024, 256), jnp.bfloat16),
        pltpu.VMEM((2, 256, 1024), jnp.bfloat16),
        pltpu.VMEM((2, 1024, 256), jnp.bfloat16),
        pltpu.VMEM((2, 1024, 256), jnp.float32),
        pltpu.VMEM((2, 1024, 128), jnp.float32),
        pltpu.SemaphoreType.DMA((SEMS,)),
        pltpu.SemaphoreType.DMA((SEMS,)),
    ]
    return pl.pallas_call(
        kernel,
        out_shape=jax.ShapeDtypeStruct(queries.shape, jnp.bfloat16),
        in_specs=[vmem, vmem, vmem, smem, vmem],
        out_specs=vmem,
        scratch_shapes=scratch,
        compiler_params=pltpu.CompilerParams(collective_id=0, has_side_effects=True, vmem_limit_bytes=56 * 2**20),
    )(queries, key_rows, value_rows, block_place, document_ids)


def solution(mesh):
    rows = P(("grp", "ctx"), None)
    return jax.shard_map(
        on_device,
        mesh=mesh,
        in_specs=(rows, rows, rows, P(("grp", "ctx")), P("grp", "ctx")),
        out_specs=rows,
        check_vma=False,
    )
```

```python
import functools
import math

import jax
import jax.numpy as jnp
from jax import lax
from jax.experimental import pallas as pl
from jax.experimental.pallas import tpu as pltpu
from jax.sharding import PartitionSpec as P

MESH = pl.DeviceIdType.MESH

DH = 128
BLK = 128
ROWS = 528
AUX = 512
CUT = 256
HALF = {"a": (0, 128, CUT), "b": (CUT, 400, ROWS)}
COLS = 9
BIG = 2.0**126


ORDER = (
    ("forward", 0, "a", 0),
    ("along_y", 0, "a"),
    ("forward", 0, "b", 0),
    ("along_y", 0, "b"),
    ("take_a", 4),
    ("pass_y", 0, "b"),
    ("pair",),
    ("take_b", 4, 0),
    ("take_a", 8),
    ("take_a", 1),
    ("pass_y", 0, "a"),
    ("third",),
    ("take_b", 1, 0),
    ("pass_y", 4, "a"),
    ("take_b", 4, -1),
    ("take_b", 4, 1),
    ("tail", 0, "b"),
    ("pass_y", 1, "a"),
    ("tail", 0, "a"),
    ("take_a", 3),
    ("tail", 4, "a"),
    ("take_b", 3, 0),
    ("take_b", 4, 2),
    ("tail", 1, "a"),
    ("tail", 4, "b"),
    ("comp", (0,), 0),
    ("take_b", 1, 1),
    ("take_a", 7),
    ("take_b", 8, 0),
    ("pass_y", 8, "a"),
    ("take_a", 5),
    ("take_b", 1, -1),
    ("pass_y", 3, "a"),
    ("take_a", 2),
    ("comp", (0,), 1),
    ("take_b", 1, 2),
    ("tail", 1, "b"),
    ("take_b", 8, 1),
    ("take_b", 8, 2),
    ("take_b", 3, -1),
    ("comp", (1, 4), 0),
    ("take_b", 3, 1),
    ("tail", 3, "a"),
    ("take_b", 8, -1),
    ("pass_y", 5, "a"),
    ("tail", 8, "a"),
    ("take_b", 3, 2),
    ("take_a", 6),
    ("pass_y", 7, "a"),
    ("tail", 3, "b"),
    ("tail", 8, "b"),
    ("pass_y", 2, "a"),
    ("take_b", 2, -1),
    ("take_b", 7, 0),
    ("comp", (1, 4), 1),
    ("take_b", 7, 1),
    ("take_b", 2, 0),
    ("take_b", 2, 1),
    ("take_b", 5, 2),
    ("take_b", 5, 1),
    ("take_b", 5, 0),
    ("comp", (3, 8), 0),
    ("take_b", 5, -1),
    ("take_b", 6, -1),
    ("take_b", 7, 2),
    ("take_b", 2, 2),
    ("tail", 2, "a"),
    ("take_b", 6, 0),
    ("tail", 5, "a"),
    ("tail", 5, "b"),
    ("pass_y", 6, "a"),
    ("comp", (3, 8), 1),
    ("take_b", 7, -1),
    ("tail", 7, "b"),
    ("take_b", 6, 1),
    ("tail", 2, "b"),
    ("comp", (5,), 0),
    ("take_b", 6, 2),
    ("tail", 6, "a"),
    ("comp", (5,), 1),
    ("tail", 7, "a"),
    ("tail", 6, "b"),
    ("comp", (2,), 0),
    ("comp", (2,), 1),
    ("comp", (6, 7), 0),
    ("comp", (6, 7), 1),
)


def rows_of(part):
    first, _, last = HALF[part]
    return pl.ds(first, last - first)


def kernel(q_ref, k_ref, v_ref, place_ref, docs_ref, out_ref, *scratch):
    bufs = scratch[:COLS]
    qa, kb, vb, acc, top, send_sems, recv_sems = scratch[COLS:]
    y = lax.axis_index("grp")
    rank = lax.axis_index("ctx")
    x, z, core = lax.div(rank, 8), lax.rem(lax.div(rank, 2), 4), lax.rem(rank, 2)
    chip = x * 4 + z

    xs, ys, zs = ([lax.rem(v + k, 4) for k in range(4)] for v in (x, y, z))
    here = {(a, c): (xs[a] * 4 + zs[c]) * 2 + core for a, c in ((0, 0), (1, 0), (3, 0), (0, 1), (0, 2), (0, 3))}
    partner = chip * 2 + 1 - core

    def device(dx=0, dy=0, dz=0, flip=False):
        return (ys[dy % 4], partner if flip else here[dx % 4, dz % 4])

    friends = [dict(dx=1), dict(dx=-1), dict(dy=1), dict(dy=-1), dict(dz=1), dict(dz=-1), dict(dz=2), dict(flip=True)]
    barrier = pltpu.get_barrier_semaphore()
    for friend in friends:
        pl.semaphore_signal(barrier, inc=1, device_id=device(**friend), device_id_type=MESH)

    mine = bufs[0]
    mine[core, y, pl.ds(0, 128), :] = k_ref[0:128, :].T
    mine[core, y, pl.ds(128, 128), :] = k_ref[128:256, :].T
    mine[core, y, pl.ds(256, 256), :] = v_ref[...]
    row_at = lax.broadcasted_iota(jnp.int32, (16, 128), 0)
    aux = jnp.where(
        row_at == 0,
        docs_ref[0:1, 0:128],
        jnp.where(
            row_at == 1,
            docs_ref[0:1, 128:256],
            jnp.where(row_at == 2, place_ref[0], jnp.where(row_at == 3, place_ref[1], 0)),
        ),
    )
    mine[core, y, pl.ds(AUX, 16), :] = aux.astype(jnp.float32).astype(jnp.bfloat16)

    index_of = {}

    def sem_at(key):
        return index_of.setdefault(key, len(index_of))

    def active(d):
        return chip >= d

    sent = []

    def copy(key, src_d, dst_d, slot, rows, to):
        at = sem_at(key)
        return pltpu.make_async_remote_copy(
            src_ref=bufs[src_d].at[core, slot, rows, :],
            dst_ref=bufs[dst_d].at[core, slot, rows, :],
            send_sem=send_sems.at[at],
            recv_sem=recv_sems.at[at],
            device_id=to,
            device_id_type=MESH,
        )

    def send(key, src_d, dst_d, slot, rows, to, cond):
        c = copy(key, src_d, dst_d, slot, rows, to)

        @pl.when(cond)
        def _():
            c.start()

        sent.append((c, cond))

    waited = set()

    def receive(key, d, slot, rows, cond):
        if key in waited:
            return
        waited.add(key)
        c = copy(key, d, d, slot, rows, device(dx=1))

        @pl.when(cond)
        def _():
            c.wait_recv()

    def slot_of(k):
        return ys[k % 4]

    def along_y(d, part):
        for step in (1, -1):
            send(("y", d, part, step), d, d, y, rows_of(part), device(dy=step), active(d))

    def half(part, step):
        first, mid, last = HALF[part]
        return pl.ds(first, mid - first) if step == 1 else pl.ds(mid, last - mid)

    def pass_y(d, part):
        for step in (1, -1):
            receive(("y", d, part, step), d, slot_of(-step), rows_of(part), active(d))
            send(("yf", d, part, step), d, d, slot_of(-step), half(part, step), device(dy=step), active(d))

    def last_y(d, part):
        for step in (1, -1):
            receive(("yf", d, part, step), d, slot_of(2), half(part, step), active(d))

    def along_x(d, part, k):
        send(("x", d + 4, part, k), d, d + 4, slot_of(k), rows_of(part), device(dx=1), active(d) & (x <= 2))

    def along_z(d, part, k):
        for delta in (1, 3, 2):
            straight = z + delta <= 3
            to = device(dz=delta)
            for wrap in (False, True):
                dst = d + delta - (4 if wrap else 0)
                if dst < 0 or dst > 7 or dst == 6:
                    continue
                ok = active(d) & (jnp.logical_not(straight) if wrap else straight)
                send(("z", dst, part, k), d, dst, slot_of(k), rows_of(part), to, ok)

    def came_by(d):
        return "x" if d in (4, 8, 6) else "z"

    def forward(d, part, k):
        if d in (0, 4, 2):
            along_x(d, part, k)
        if d in (0, 4, 8):
            along_z(d, part, k)

    def take(d, part, k):
        receive((came_by(d), d, part, k), d, slot_of(k), rows_of(part), active(d))

    def take_a(d):
        take(d, "a", 0)
        along_y(d, "a")
        forward(d, "a", 0)

    def take_b(d, k):
        take(d, "b", k)
        forward(d, "b", k)

    def core_copy(d, part, slot):
        at = sem_at(("c", d, part))
        piece = bufs[d].at[slot, :, rows_of(part), :]
        return pltpu.make_async_remote_copy(
            src_ref=piece,
            dst_ref=piece,
            send_sem=send_sems.at[at],
            recv_sem=recv_sems.at[at],
            device_id=device(flip=True),
            device_id_type=MESH,
        )

    def swap(d, part):
        c = core_copy(d, part, core)

        @pl.when(active(d))
        def _():
            c.start()

        sent.append((c, active(d)))

    def swapped(d):
        for part in ("a", "b"):
            c = core_copy(d, part, 1 - core)
            pl.when(active(d))(c.wait_recv)

    factor = DH**-0.5 * math.log2(math.e)

    def stage(d, base):
        buf = bufs[d]
        groups = [place_ref[j] // 2 for j in range(2)]
        entry = lax.broadcasted_iota(jnp.int32, (128, 128), 0).astype(jnp.float32)
        for c in range(2):
            auxes = [buf[c, i, pl.ds(AUX, 16), :].astype(jnp.float32) for i in range(4)]
            wanted = [(j, s) for j in range(2) for s in range(2)]
            picks = {}
            for i in range(4):
                for b in range(2):
                    place = auxes[i][2 + b : 3 + b, :]
                    for j, s in wanted:
                        hit = place == (groups[j] * 2 + s).astype(jnp.float32)
                        picks[i, b, j, s] = hit.astype(jnp.float32).astype(jnp.bfloat16)
            for first, ref in ((0, kb), (256, vb)):
                found = {w: None for w in wanted}
                for i in range(4):
                    for b in range(2):
                        block = buf[c, i, pl.ds(first + b * 128, 128), :]
                        for w in wanted:
                            term = block * picks[(i, b) + w]
                            found[w] = term if found[w] is None else found[w] + term
                for j, s in wanted:
                    at = pl.ds(base + (c * 2 + s) * 128, 128)
                    if first == 0:
                        kb[j, pl.ds(0, 128), at] = found[j, s]
                    else:
                        vb[j, at, pl.ds(0, 128)] = found[j, s]
            for j, s in wanted:
                labels = auxes[0][s : s + 1, :]
                for i in range(1, 4):
                    labels = jnp.where(groups[j] == i, auxes[i][s : s + 1, :], labels)
                at = pl.ds(base + (c * 2 + s) * 128, 128)
                kb[j, pl.ds(128, 128), at] = jnp.where(entry == labels, 0.0, -BIG).astype(jnp.bfloat16)

    step_rows = 512

    def attend(ds, j):
        n_keys = 512 * len(ds)

        def score(i):
            rows = pl.ds(i * step_rows, step_rows)
            scores = jnp.dot(qa[j, rows, :], kb[j, :, 0:n_keys], preferred_element_type=jnp.float32)
            if 0 in ds:
                q_pos = core * 256 + (place_ref[j] % 2) * 128 + lax.broadcasted_iota(jnp.int32, (step_rows, n_keys), 0) % 128
                k_pos = lax.broadcasted_iota(jnp.int32, (step_rows, n_keys), 1)
                scores = jnp.where(k_pos <= q_pos, scores, -BIG)
            return scores

        def rest(i, scores):
            rows = pl.ds(i * step_rows, step_rows)
            high = jnp.max(scores, axis=1, keepdims=True)
            first = 0 in ds
            new = jnp.broadcast_to(high, (step_rows, 128)) if first else jnp.maximum(top[j, rows, :], high)
            weights = jnp.exp2((scores - new[:, 0:1]) * factor).astype(jnp.bfloat16)
            got = jnp.dot(weights, vb[j, 0:n_keys, :], preferred_element_type=jnp.float32)
            if first:
                acc[j, rows, :] = got
            else:
                ratio = jnp.exp2((top[j, rows, :] - new) * factor)
                acc[j, rows, 0:128] = acc[j, rows, 0:128] * ratio + got[:, 0:128]
                acc[j, rows, 128:256] = acc[j, rows, 128:256] * ratio + got[:, 128:256]
            top[j, rows, :] = new

        n = 1024 // step_rows
        now = score(0)
        for i in range(n):
            later = score(i + 1) if i + 1 < n else None
            rest(i, now)
            now = later

    def compute(ds, j):
        def some(ds):
            if j == 0:
                for e, d in enumerate(ds):
                    stage(d, 512 * e)
            attend(ds, j)

        if len(ds) == 1:
            pl.when(active(ds[0]))(lambda: some(ds))
        else:
            pl.when(active(ds[1]))(lambda: some(ds))
            pl.when(active(ds[0]) & jnp.logical_not(active(ds[1])))(lambda: some(ds[:1]))

    def ready():
        for j in range(2):
            group, s = place_ref[j] // 2, place_ref[j] % 2
            labels = jnp.zeros((1, 128), jnp.float32)
            for i in range(4):
                tile = bufs[0][core, i, pl.ds(AUX, 16), :].astype(jnp.float32)
                for slot in range(2):
                    labels = jnp.where((group == i) & (s == slot), tile[slot : slot + 1, :], labels)
            column = jnp.broadcast_to(labels, (128, 128)).T
            entry = lax.broadcasted_iota(jnp.int32, (128, 128), 1).astype(jnp.float32)
            hot = jnp.where(entry == column, 1.0, 0.0).astype(jnp.bfloat16)
            for h in range(8):
                qa[j, pl.ds(h * 128, 128), pl.ds(128, 128)] = hot

    pl.semaphore_wait(barrier, len(friends))

    def local():
        for j in range(2):
            for h in range(8):
                qa[j, pl.ds(h * 128, 128), pl.ds(0, 128)] = q_ref[pl.ds(j * 128, 128), pl.ds(h * 128, 128)]
        vb[:, :, pl.ds(128, 128)] = jnp.ones((2, 1024, 128), jnp.bfloat16)

    def tail(d, part):
        if part == "a":
            last_y(d, "a")
        swap(d, part)

    def pair():
        forward(0, "b", 1)
        forward(0, "b", -1)

    def third():
        last_y(0, "b")
        forward(0, "b", 2)

    def comp(ds, j):
        if j == 0:
            for d in ds:
                swapped(d)
            if 0 in ds:
                ready()
        compute(ds, j)

    steps = dict(
        along_y=along_y, pass_y=pass_y, forward=forward, take_a=take_a, take_b=take_b, tail=tail, pair=pair, third=third, comp=comp
    )
    for at, (name, *args) in enumerate(ORDER):
        if at == 4:
            local()
        steps[name](*args)

    for j in range(2):
        for h in range(8):
            rows = pl.ds(h * 128, 128)
            result = acc[j, rows, 0:128] / acc[j, rows, 128:256]
            out_ref[pl.ds(j * 128, 128), pl.ds(h * 128, 128)] = result.astype(jnp.bfloat16)

    for c, cond in sent:
        pl.when(cond)(c.wait_send)
    assert len(index_of) <= SEMS, len(index_of)


SEMS = 128


def on_device(queries, key_rows, value_rows, block_place, document_ids):
    vmem = pl.BlockSpec(memory_space=pltpu.VMEM)
    smem = pl.BlockSpec(memory_space=pltpu.SMEM)
    scratch = [pltpu.VMEM((2, 4, ROWS, 128), jnp.bfloat16) for _ in range(COLS)]
    scratch += [
        pltpu.VMEM((2, 1024, 256), jnp.bfloat16),
        pltpu.VMEM((2, 256, 1024), jnp.bfloat16),
        pltpu.VMEM((2, 1024, 256), jnp.bfloat16),
        pltpu.VMEM((2, 1024, 256), jnp.float32),
        pltpu.VMEM((2, 1024, 128), jnp.float32),
        pltpu.SemaphoreType.DMA((SEMS,)),
        pltpu.SemaphoreType.DMA((SEMS,)),
    ]
    return pl.pallas_call(
        kernel,
        out_shape=jax.ShapeDtypeStruct(queries.shape, jnp.bfloat16),
        in_specs=[vmem, vmem, vmem, smem, vmem],
        out_specs=vmem,
        scratch_shapes=scratch,
        compiler_params=pltpu.CompilerParams(collective_id=0, has_side_effects=True, vmem_limit_bytes=56 * 2**20),
    )(queries, key_rows, value_rows, block_place, document_ids)


def solution(mesh):
    rows = P(("grp", "ctx"), None)
    return jax.shard_map(
        on_device,
        mesh=mesh,
        in_specs=(rows, rows, rows, P(("grp", "ctx")), P("grp", "ctx")),
        out_specs=rows,
        check_vma=False,
    )
```
